128 devices in a mesh: fsdp: 32 (over y, z, x_lo), mp: 4 (over x_hi, core).
Axes of the slice: x: 4 (x_hi: 2, x_lo: 2; x = x_hi * 2 + x_lo), y: 4, z: 4, core: 2. Of those that a mesh axis runs over, the one named last changes fastest.
Arguments:
- tokens: bfloat16 [4096, 8192], P('fsdp'), may hold values from -22 to 22
- cotangent: bfloat16 [4096, 16384], P('fsdp', 'mp'), may hold values from -22 to 22
- weight: bfloat16 [8192, 16384], P('fsdp', 'mp'), may hold values from -0.0625 to 0.0625
- row_prev: float32 [8192], P('fsdp'), may hold values from 0.01 to 0.3
- col_prev: float32 [16384], P('mp'), may hold values from 0.01 to 0.3
Outputs:
- input_grad: bfloat16 [4096, 8192], P('mp', 'fsdp')
- update: float32 [8192, 16384], P('fsdp', 'mp')
- row_next: float32 [8192], P('fsdp')
- col_next: float32 [16384], P('mp')
- update_rms: float32 [], replicated
The draws below stay inside these ranges and needn't reach their ends.
All inputs are finite; a program needn't handle non-finite values.
Results may differ from the reference program's by a relative error of at most 0.00055.
Values may be sent and summed in bfloat16 or wider, within the bound.
No kernel may reach another device: no remote copies, remote signals or barrier semaphores. Data moves between devices by JAX's collectives and lax.ppermute only.
A program may use at most 128 MiB of HBM per device.

```python
import math
import jax
import jax.numpy as jnp
from jax import lax

D = 8192
FF = 16384
TOKENS = 4096


def token_group(key):
    return jax.random.bernoulli(jax.random.fold_in(key, 5), 0.5, (TOKENS,))


def emphasis(key, token_first, width):
    column_first = jax.random.bernoulli(key, 0.25, (width,))
    agree = token_first[:, None] == column_first[None, :]
    return jnp.where(agree, 1.0, 0.25).astype(jnp.float32)


def scaled_rows(key, width, slope):
    first, second = jax.random.split(key)
    index = jnp.arange(width, dtype=jnp.float32)
    base = jnp.sqrt(1.0 + slope * index / width)
    jitter = jnp.exp(jax.random.uniform(second, (width,), jnp.float32, -1.15, 1.15))
    return (first, base * jitter)


def draw_tokens(key, part):
    token_first = token_group(key)
    key = jax.random.fold_in(key, 11)
    key, pick = jax.random.split(key)
    factor = emphasis(pick, token_first, D)
    inner, scales = scaled_rows(key, D, 2.0)
    values = jnp.clip(jax.random.normal(inner, (TOKENS, D), jnp.float32), -4.0, 4.0)
    return (values * scales[None, :] * factor).astype(jnp.bfloat16)


def draw_cotangent(key, part):
    token_first = token_group(key)
    key = jax.random.fold_in(key, 23)
    key, pick = jax.random.split(key)
    factor = emphasis(pick, token_first, FF)
    inner, scales = scaled_rows(key, FF, 2.0)
    values = jnp.clip(jax.random.normal(inner, (TOKENS, FF), jnp.float32), -4.0, 4.0)
    return (values * scales[None, :] * factor).astype(jnp.bfloat16)


def block_scale(own_key, shape, shards, low, top_value):
    def one(dim, shards_of):
        steps = jax.random.uniform(jax.random.fold_in(jax.random.fold_in(own_key, 6), dim), (shards_of,), jnp.float32, low / len(shards), top_value / len(shards))
        return jnp.repeat(jnp.exp(steps), shape[dim] // shards_of).reshape((-1,) + (1,) * (len(shape) - dim - 1))

    gain = one(*shards[0])
    for cut in shards[1:]:
        gain = gain * one(*cut)
    return gain


def normal_values(stream_key, extent, scale, reach, cuts=(), held_as=jnp.bfloat16):
    factor_of = block_scale(stream_key, extent, cuts, -0.22, 0.18) if cuts else 1.0
    drawn = jax.random.normal(stream_key, extent, jnp.float32) * scale * factor_of
    return jnp.minimum(jnp.maximum(drawn, -reach), reach).astype(held_as)


def setup_inputs(seed: int = 0) -> dict:
    streams_of = jax.random.split(jax.random.key(seed), 6)
    tokens = draw_tokens(jax.random.fold_in(streams_of[5], 71), 0)
    cotangent = draw_cotangent(jax.random.fold_in(streams_of[5], 71), 0)
    weight = normal_values(streams_of[2], (D, FF), D ** -0.5, 0.0625, ((0, 32), (1, 4)))
    row_prev = jnp.clip(jnp.exp(math.log(0.3) - 3.4011974 * jax.random.uniform(streams_of[3], (D,), jnp.float32) ** block_scale(streams_of[3], (D,), ((0, 32),), -0.2, 0.2)), 0.01, 0.3)
    col_prev = jnp.clip(jnp.exp(math.log(0.3) - 3.4011974 * jax.random.uniform(streams_of[4], (FF,), jnp.float32) ** block_scale(streams_of[4], (FF,), ((0, 4),), -0.2, 0.2)), 0.01, 0.3)
    return {"tokens": tokens, "cotangent": cotangent, "weight": weight, "row_prev": row_prev, "col_prev": col_prev}


decay_rate = 0.84
tiny_eps = 1e-30

def reference(tokens, cotangent, weight, row_prev, col_prev):
    grad = jnp.dot(tokens.T, cotangent, preferred_element_type=jnp.float32) * float(TOKENS) ** (-0.5)
    input_grad = jnp.dot(cotangent, weight.T, preferred_element_type=jnp.float32).astype(jnp.bfloat16)
    squares = grad * grad
    row_next = decay_rate * row_prev + (1.0 - decay_rate) * (lax.optimization_barrier(jnp.sum(squares, axis=1)) / FF + tiny_eps)
    col_next = decay_rate * col_prev + (1.0 - decay_rate) * (lax.optimization_barrier(jnp.sum(squares, axis=0)) / D + tiny_eps)
    row_mean = jnp.sum(row_next) / D
    raw = grad / jnp.sqrt(row_next[:, None] * col_next[None, :] / row_mean)
    update_rms = jnp.sqrt(jnp.sum(raw * raw) / (D * FF))
    update = raw / jnp.maximum(1.0, update_rms)
    return (input_grad, update, row_next, col_next, update_rms)
```

```python
import jax
import jax.numpy as jnp
from jax import lax
from jax.sharding import Mesh, PartitionSpec as P

D = 8192
FF = 16384
TOKENS = 4096
F32 = jnp.float32

decay_rate = 0.84
tiny_eps = 1e-30

AXES = ("y", "z", "xl", "xh", "c")
SIZES = (4, 4, 2, 2, 2)
SWAP = [(0, 1), (1, 0)]
DIAG = [(0, 3), (3, 0), (1, 2), (2, 1)]
CHUNKS = ((0, 1024), (1024, 1024))


def spread(value, axes, count):
    copies = jnp.broadcast_to(value[None], (count,) + value.shape)
    return lax.all_to_all(copies, axes, split_axis=0, concat_axis=0, tiled=True)


def body(tokens, cotangent, weight, row_prev, col_prev):
    xl = lax.axis_index("xl")
    xh = lax.axis_index("xh")
    c = lax.axis_index("c")
    half = cotangent.shape[1] // 2

    def mine(a, n, axis, index):
        return lax.dynamic_slice_in_dim(a, index * n, n, axis)

    own = mine(cotangent, half, 1, xl)
    other = lax.ppermute(mine(cotangent, half, 1, 1 - xl), "xl", SWAP)
    shard = jnp.stack([own, other])

    part = mine(tokens, 64, 0, c).reshape(64, 16, 512)
    xo = lax.all_to_all(part, ("y", "z"), split_axis=1, concat_axis=0, tiled=False)
    xp = lax.ppermute(xo, "xl", SWAP)
    x_mine = jnp.stack([xo, xp], 1)
    x_theirs = lax.ppermute(x_mine, "c", SWAP)
    x_lo = jnp.where(c == 0, x_mine, x_theirs)
    x_hi = jnp.where(c == 0, x_theirs, x_mine)
    x_all = jnp.stack([x_lo, x_hi], 2).reshape(4096, 2, 256)
    x_rel = jnp.where(xl == 0, x_all, x_all[:, ::-1]).reshape(4096, 512)

    w_own = mine(weight, half, 1, xl)
    w_other = lax.ppermute(mine(weight, half, 1, 1 - xl), "xl", SWAP)
    w_all = jnp.concatenate([w_own, w_other], 0)

    grads, rows, cols, received, partial = [], [], [], [], None
    for first, width in CHUNKS:
        piece = lax.slice_in_dim(shard, first, first + width, axis=2)
        c_all = lax.all_gather(piece, ("y", "z"), axis=0, tiled=False).reshape(4096, width)
        g = lax.dot_general(x_rel, c_all, (((0,), (0,)), ((), ())), preferred_element_type=F32)
        g = g * float(TOKENS) ** (-0.5)
        squares = g * g
        rows.append(jnp.sum(squares, axis=1))
        cols.append(jnp.sum(squares, axis=0))
        grads.append(g)
        received.append(lax.ppermute(g[256:], "xl", SWAP))
        w = lax.slice_in_dim(w_all, first, first + width, axis=1)
        term = lax.dot_general(c_all, w, (((1,), (1,)), ((), ())), preferred_element_type=F32)
        partial = term if partial is None else partial + term

    def flip(v):
        return jnp.where(xl == 0, v, jnp.concatenate([v[256:], v[:256]]))

    row_all = jnp.sum(spread(flip(sum(rows)), ("xl", "xh", "c"), 8), 0)
    row_sum = flip(row_all)
    row_prev_other = lax.ppermute(row_prev, "xl", SWAP)
    row_next = decay_rate * jnp.concatenate([row_prev, row_prev_other]) + (1.0 - decay_rate) * (
        row_sum / FF + tiny_eps
    )
    col_sum = jnp.sum(spread(jnp.concatenate(cols), ("y", "z"), 16), 0)
    col_prev_mine = mine(col_prev, half, 0, xl)
    col_half = decay_rate * col_prev_mine + (1.0 - decay_rate) * (col_sum / D + tiny_eps)
    col_other = lax.ppermute(col_half, "xl", SWAP)

    s = jnp.zeros((), F32)
    for (first, width), g in zip(CHUNKS, grads):
        s = s + jnp.sum((g * g) / (row_next[:, None] * col_half[None, first : first + width]))
    rows_own = jnp.sum(row_next[:256])
    lane = lax.broadcasted_iota(jnp.int32, (128,), 0)
    pair = jnp.where(lane == 0, s, jnp.where(lane == 1, rows_own, 0.0))
    totals = jnp.sum(spread(pair, AXES, 128), 0)
    row_mean = totals[1] / 4.0 / D
    update_rms = jnp.sqrt(row_mean * (totals[0] / (D * FF)))
    scale = jnp.sqrt(row_mean) / jnp.maximum(1.0, update_rms)

    row_own = row_next[:256]
    g_mine = jnp.concatenate([g[:256] for g in grads], 1) / jnp.sqrt(row_own[:, None] * col_half[None, :]) * scale
    g_recv = jnp.concatenate(received, 1) / jnp.sqrt(row_own[:, None] * col_other[None, :]) * scale
    update = jnp.where(
        xl == 0, jnp.concatenate([g_mine, g_recv], 1), jnp.concatenate([g_recv, g_mine], 1)
    )
    col_next = jnp.where(
        xl == 0, jnp.concatenate([col_half, col_other]), jnp.concatenate([col_other, col_half])
    )

    blocks = partial.reshape(2, 2, 1024, 512)
    keep = lax.dynamic_index_in_dim(blocks, c, 1, keepdims=False)
    send = lax.dynamic_index_in_dim(blocks, 1 - c, 1, keepdims=False)
    chip = keep + lax.ppermute(send, "c", SWAP)

    def turn(v):
        v = v.reshape(4, 2, 128, 2, 256)
        return v[:, ::-1, :, ::-1].reshape(1024, 512)

    keep = lax.dynamic_index_in_dim(chip, xh, 0, keepdims=False)
    send = lax.dynamic_index_in_dim(chip, 1 - xh, 0, keepdims=False)
    two = keep + turn(lax.ppermute(send, ("xl", "xh"), DIAG))
    got = lax.ppermute(two[:, 256:], "xl", SWAP).reshape(4, 2, 128, 256)[:, ::-1]
    total = two[:, :256].reshape(4, 2, 128, 256) + got
    total = jnp.where(xl == 0, total, total[:, ::-1]).reshape(1024, 256)
    return (total.astype(jnp.bfloat16), update, row_own, col_next, update_rms)


def solution(mesh):
    fine = Mesh(mesh.devices.reshape(SIZES), AXES)
    fsdp, mp = ("y", "z", "xl"), ("xh", "c")
    in_specs = (P(fsdp, None), P(fsdp, mp), P(fsdp, mp), P(fsdp), P(mp))
    out_specs = (P(mp, fsdp), P(fsdp, mp), P(fsdp), P(mp), P())
    return jax.shard_map(body, mesh=fine, in_specs=in_specs, out_specs=out_specs, check_vma=False)
```

```python
import math

import jax
import jax.numpy as jnp
from jax import lax
from jax.experimental import pallas as pl
from jax.experimental.pallas import tpu as pltpu
from jax.sharding import Mesh, PartitionSpec as P

D = 8192
FF = 16384
TOKENS = 4096
F32 = jnp.float32
BF16 = jnp.bfloat16

decay_rate = 0.84
tiny_eps = 1e-30

AXES = ("y", "z", "xl", "xh", "c")
SIZES = (4, 4, 2, 2, 2)
SWAP = [(0, 1), (1, 0)]
DIAG = [(0, 3), (3, 0), (1, 2), (2, 1)]
WIDE = 1024
MIB = 1 << 20
SHORT = pl.CostEstimate(flops=1, bytes_accessed=1, transcendentals=0)
LONG = pl.CostEstimate(flops=2 * 10**10, bytes_accessed=1, transcendentals=0)


def spread(value, axes, count):
    copies = jnp.broadcast_to(value[None], (count,) + value.shape)
    return lax.all_to_all(copies, axes, split_axis=0, concat_axis=0, tiled=True)


def mine(a, n, axis, index):
    return lax.dynamic_slice_in_dim(a, index * n, n, axis)


def shift(a, axis, k):
    return lax.ppermute(a, axis, [(i, (i + k) % 4) for i in range(4)])


def near_three(start, axis):
    return [shift(start, axis, 1), shift(start, axis, 3), shift(start, axis, 2)]


def spread_pieces(start, three, then):
    a, b, c = three
    p, q = jnp.concatenate([start, a]), jnp.concatenate([b, c])
    p1, q3 = shift(p, then, 1), shift(q, then, 3)
    q1, p3 = shift(q, then, 1), shift(p, then, 3)
    p2, q2 = shift(p1, then, 1), shift(q3, then, 3)
    pieces = [p, q, p1, q1, p3, q3, p2, q2]
    places = []
    for d in (0, 1, 3, 2):
        places += [(0, d), (1, d), (3, d), (2, d)]
    return pieces, places


def transposed_tokens(where, blocks):
    def kernel(where_ref, a_ref, b_ref, c_ref, d_ref, out_ref, hold):
        own_x, own_c = where_ref[0] * 128, where_ref[2] * 64
        other_x, other_c = 128 - own_x, 64 - own_c
        for ref, row in (
            (a_ref, own_x + own_c),
            (b_ref, other_x + own_c),
            (c_ref, own_x + other_c),
            (d_ref, other_x + other_c),
        ):
            hold[pl.ds(pl.multiple_of(row, 64), 64), :] = ref[0]
        out_ref[...] = hold[...].T

    block = pl.BlockSpec((1, 64, 512), lambda i, where_ref: (i, 0, 0))
    return pl.pallas_call(
        kernel,
        grid_spec=pltpu.PrefetchScalarGridSpec(
            num_scalar_prefetch=1,
            grid=(16,),
            in_specs=[block] * 4,
            out_specs=pl.BlockSpec((512, 256), lambda i, where_ref: (0, i)),
            scratch_shapes=[pltpu.VMEM((256, 512), BF16)],
        ),
        out_shape=jax.ShapeDtypeStruct((512, TOKENS), BF16),
        cost_estimate=LONG,
    )(where, *blocks)


def squares_of(g, row_ref, col_ref, columns, first):
    squares = g * g
    rows, width = g.shape
    col_ref[:, columns] = jnp.sum(squares.reshape(rows // 8, 8, width), 0)
    sums = squares[:, :128]
    for k in range(128, width, 128):
        sums = sums + squares[:, k : k + 128]
    if first is True:
        row_ref[...] = sums
    else:
        row_ref[...] += sums


def grad_shapes(width):
    return (
        jax.ShapeDtypeStruct((256, width), F32),
        jax.ShapeDtypeStruct((2, 256, width // 2), F32),
        jax.ShapeDtypeStruct((512, 128), F32),
        jax.ShapeDtypeStruct((8, width), F32),
    )


def own_other(a, first, axis):
    low, high = (a[:256], a[256:]) if axis == 0 else (a[:, :256], a[:, 256:])
    return jnp.where(first, low, high), jnp.where(first, high, low)


def gradient_of_pieces(xt, pieces, index, xl):
    width = pieces[0].shape[1]
    n = 2 * len(pieces)
    tile = 256

    def kernel(xl_ref, index_ref, xt_ref, *refs):
        ins = refs[: len(pieces)]
        c_ref, own_ref, other_ref, row_ref, col_ref, hold, in_sems, out_sem = refs[len(pieces) :]
        copies = []
        for k in range(n):
            copies.append(
                pltpu.make_async_copy(
                    ins[k // 2].at[pl.ds(128 * (k % 2), 128)], hold.at[index_ref[k]], in_sems.at[k]
                )
            )
            copies[-1].start()
        for copy in copies:
            copy.wait()
        write = pltpu.make_async_copy(hold, c_ref, out_sem)
        write.start()
        for first in range(0, width, tile):
            block = hold[:, :, first : first + tile].reshape(TOKENS, tile)
            g = jnp.dot(xt_ref[...], block, preferred_element_type=F32) * float(TOKENS) ** (-0.5)
            own, other = own_other(g, xl_ref[0] == 0, 0)
            own_ref[:, first : first + tile] = own
            part, place = divmod(first, width // 2)
            other_ref[part, :, place : place + tile] = other
            squares_of(g, row_ref, col_ref, slice(first, first + tile), first == 0)
        write.wait()

    vmem = pl.BlockSpec(memory_space=pltpu.VMEM)
    anywhere = pl.BlockSpec(memory_space=pl.ANY)
    smem = pl.BlockSpec(memory_space=pltpu.SMEM)
    out = pl.pallas_call(
        kernel,
        out_shape=(jax.ShapeDtypeStruct((n, 128, width), BF16),) + grad_shapes(width),
        in_specs=[smem, smem, vmem] + [anywhere] * len(pieces),
        out_specs=(anywhere,) + (vmem,) * 4,
        scratch_shapes=[
            pltpu.VMEM((n, 128, width), BF16),
            pltpu.SemaphoreType.DMA((n,)),
            pltpu.SemaphoreType.DMA,
        ],
        compiler_params=pltpu.CompilerParams(vmem_limit_bytes=56 * MIB),
        cost_estimate=SHORT,
    )(xl, index, xt, *pieces)
    return (out[0].reshape(TOKENS, width),) + tuple(out[1:])


def gradient(xt, c_all, xl):
    width = c_all.shape[1]
    tile = 256

    def kernel(xl_ref, xt_ref, c_ref, own_ref, other_ref, row_ref, col_ref):
        g = jnp.dot(xt_ref[...], c_ref[...], preferred_element_type=F32) * float(TOKENS) ** (-0.5)
        own_ref[...], other_ref[0] = own_other(g, xl_ref[0] == 0, 0)

        @pl.when(pl.program_id(0) == 0)
        def _():
            row_ref[...] = jnp.zeros_like(row_ref)

        squares_of(g, row_ref, col_ref, slice(None), False)

    return pl.pallas_call(
        kernel,
        grid=(width // tile,),
        out_shape=grad_shapes(width),
        in_specs=[
            pl.BlockSpec(memory_space=pltpu.SMEM),
            pl.BlockSpec((512, TOKENS), lambda j: (0, 0)),
            pl.BlockSpec((TOKENS, tile), lambda j: (0, j)),
        ],
        out_specs=(
            pl.BlockSpec((256, tile), lambda j: (0, j)),
            pl.BlockSpec((1, 256, tile), lambda j: (j // (width // tile // 2), 0, j % (width // tile // 2))),
            pl.BlockSpec((512, 128), lambda j: (0, 0)),
            pl.BlockSpec((8, tile), lambda j: (0, j)),
        ),
        compiler_params=pltpu.CompilerParams(vmem_limit_bytes=56 * MIB),
        cost_estimate=SHORT,
    )(xl, xt, c_all)


NT = (((1,), (1,)), ((), ()))


def terms(where, far, c_1, c_2, w_all, received=None):
    w1, w2 = c_1.shape[1], c_2.shape[1]
    keep = received is not None

    def kernel(where_ref, c1_ref, c2_ref, w_ref, *refs):
        t = lax.dot_general(c1_ref[...], w_ref[:, :w1], NT, preferred_element_type=F32) + lax.dot_general(
            c2_ref[...], w_ref[:, w1:], NT, preferred_element_type=F32
        )
        if not keep:
            refs[0][...] = t
            return
        got_ref, both, own, other = refs
        t = t + got_ref[...]

        @pl.when(pl.program_id(0) == 0)
        def _():
            both[:, :256], both[:, 256:] = own_other(t, where_ref[0] == 0, 1)

        @pl.when(pl.program_id(0) == 1)
        def _():
            own[...], other[...] = own_other(t, where_ref[0] == 0, 1)

    def rows(i, where_ref):
        high = 1 - where_ref[1] if far else where_ref[1]
        core = where_ref[2] if keep else 1 - where_ref[2]
        return ((2 * high + core) * 2 + i, 0)

    step = pl.BlockSpec((512, 512), lambda i, where_ref: (i, 0))
    block = jax.ShapeDtypeStruct((512, 256), F32)
    whole = [pl.BlockSpec((512, n), lambda i, where_ref: (0, 0)) for n in (512, 256, 256)]
    return pl.pallas_call(
        kernel,
        grid_spec=pltpu.PrefetchScalarGridSpec(
            num_scalar_prefetch=1,
            grid=(2,),
            in_specs=[
                pl.BlockSpec((512, w1), rows),
                pl.BlockSpec((512, w2), rows),
                pl.BlockSpec((512, w1 + w2), lambda i, where_ref: (0, 0)),
            ]
            + [step] * keep,
            out_specs=whole if keep else step,
        ),
        out_shape=[jax.ShapeDtypeStruct((512, 512), F32), block, block]
        if keep
        else jax.ShapeDtypeStruct((1024, 512), F32),
        compiler_params=pltpu.CompilerParams(vmem_limit_bytes=56 * MIB),
        cost_estimate=SHORT,
    )(where, c_1, c_2, w_all, *((received,) if keep else ()))


def clipped(where, scale, row_factor, own, received, own_factors, received_factors):
    half = sum(g.shape[1] for g in own)
    tile = math.gcd(*(g.shape[1] for g in own + received))
    steps = half // tile
    blocks, counts = list(own) + list(received), [g.shape[1] // tile for g in own + received]
    starts = [sum(counts[:k]) for k in range(len(counts))]

    def kernel(where_ref, scale_ref, row_ref, col_ref, *refs):
        out_ref = refs[-1]
        j = pl.program_id(0)
        for ref, start, count in zip(refs, starts, counts):

            @pl.when(jnp.logical_and(j >= start, j < start + count))
            def _():
                out_ref[...] = ref[...] * (row_ref[...] * scale_ref[0]) * col_ref[...]

    def spec(start, count):
        return pl.BlockSpec((256, tile), lambda j, where_ref: (0, jnp.clip(j - start, 0, count - 1)))

    def place(j, where_ref):
        own_half = jnp.where(j < steps, where_ref[0], 1 - where_ref[0])
        return (0, own_half * steps + j % steps)

    return pl.pallas_call(
        kernel,
        grid_spec=pltpu.PrefetchScalarGridSpec(
            num_scalar_prefetch=1,
            grid=(2 * steps,),
            in_specs=[
                pl.BlockSpec(memory_space=pltpu.SMEM),
                pl.BlockSpec((256, 1), lambda j, where_ref: (0, 0)),
                pl.BlockSpec((1, tile), lambda j, where_ref: (0, j)),
            ]
            + [spec(s, n) for s, n in zip(starts, counts)],
            out_specs=pl.BlockSpec((256, tile), place),
        ),
        out_shape=jax.ShapeDtypeStruct((256, 2 * half), F32),
        compiler_params=pltpu.CompilerParams(vmem_limit_bytes=56 * MIB),
        cost_estimate=SHORT,
    )(
        where,
        scale.reshape(1),
        row_factor[:, None],
        jnp.concatenate([own_factors, received_factors])[None, :],
        *blocks,
    )


def body(tokens, cotangent, weight, row_prev, col_prev):
    y, z = lax.axis_index("y"), lax.axis_index("z")
    xl, xh, c = lax.axis_index("xl"), lax.axis_index("xh"), lax.axis_index("c")
    half = cotangent.shape[1] // 2
    first_xl = xl == 0
    after = lax.optimization_barrier

    where = jnp.stack([xl, xh, c]).astype(jnp.int32)

    away = mine(cotangent, half, 1, 1 - xl)
    part, away = after((mine(tokens, 64, 0, c), away))
    other = lax.ppermute(away, "xl", SWAP)
    part = part.reshape(64, 16, 512)
    xo = lax.all_to_all(part, ("y", "z"), split_axis=1, concat_axis=0, tiled=False)

    own = mine(cotangent, half, 1, xl)
    row_prev_other = lax.ppermute(row_prev, "xl", SWAP)
    own, other, xo, row_prev_other = after((own, other, xo, row_prev_other))
    own_1, own_2 = own[:, :WIDE], own[:, WIDE:]
    other_1, other_2 = other[:, :WIDE], other[:, WIDE:]
    shard = jnp.where(first_xl, jnp.stack([own_2, other_2]), jnp.stack([other_2, own_2]))
    c_2 = lax.all_gather(shard, ("y", "z"), axis=0, tiled=False).reshape(TOKENS, half - WIDE)
    pieces, places = spread_pieces(own_1, near_three(own_1, "y"), "z")
    index = [((y - dy) % 4 * 4 + (z - dz) % 4) * 2 + xl for dy, dz in places]
    more, places = spread_pieces(other_1, near_three(other_1, "z"), "y")
    index += [((y - dy) % 4 * 4 + (z - dz) % 4) * 2 + 1 - xl for dz, dy in places]

    xp = lax.ppermute(xo, "xl", SWAP)
    to = lax.ppermute(xo, "c", SWAP)
    near = [pieces[2], pieces[5], more[2], more[5]]
    xp, near = after((xp, near))
    pieces[2], pieces[5], more[2], more[5] = near
    tp = lax.ppermute(xp, "c", SWAP)
    xt = transposed_tokens(where, (xo, xp, to, tp))
    w_own = mine(weight, half, 1, xl)
    w_other = lax.ppermute(mine(weight, half, 1, 1 - xl), "xl", SWAP)
    w_all = jnp.where(first_xl, jnp.concatenate([w_own, w_other]), jnp.concatenate([w_other, w_own]))
    w_all, xt, last = after((w_all, xt, pieces[6:] + more[6:]))
    pieces[6:], more[6:] = last[:2], last[2:]

    c_1, g_1, send_1, rows_1, cols_1 = gradient_of_pieces(
        xt, pieces + more, jnp.stack(index).astype(jnp.int32), where
    )
    received_1a = lax.ppermute(send_1[0], "xl", SWAP)
    received_1b = lax.ppermute(send_1[1], "xl", SWAP)
    w_all, _ = after((w_all, rows_1))
    far_terms = terms(where, True, c_1, c_2, w_all)
    far_core = lax.ppermute(far_terms, "c", SWAP)
    xt, _ = after((xt, far_terms))
    g_2, send_2, rows_2, cols_2 = gradient(xt, c_2, where)
    received_2 = lax.ppermute(send_2, "xl", SWAP)

    cols = jnp.sum(jnp.concatenate([cols_1, cols_2], 1), 0)
    cols, received_1a = after((cols, received_1a))
    col_sum = jnp.sum(spread(cols, ("y", "z"), 16), 0)
    w_all, _ = after((w_all, rows_2))
    near_terms = terms(where, False, c_1, c_2, w_all)
    near_core = lax.ppermute(near_terms, "c", SWAP)
    col_prev_mine = mine(col_prev, half, 0, xl)
    col_half = decay_rate * col_prev_mine + (1.0 - decay_rate) * (col_sum / D + tiny_eps)

    def over_columns(g, col):
        return jnp.sum(g * g * (1.0 / col)[None, :], 1)

    col_1, col_2 = col_half[:WIDE], col_half[WIDE:]
    over_own = over_columns(g_1, col_1) + over_columns(g_2, col_2)
    over_other, first = 0.0, 0
    for g in (send_1[0], send_1[1], send_2[0], send_2[1]):
        over_other = over_other + over_columns(g, col_half[first : first + g.shape[1]])
        first += g.shape[1]
    plain = jnp.sum(rows_1 + rows_2, 1)
    plain_own, plain_other = own_other(plain, first_xl, 0)
    sums = jnp.stack([plain_own, over_own, plain_other, over_other])
    sums, received_1b = after((sums, received_1b))
    seen = spread(sums, ("xl", "xh", "c"), 8).reshape(2, 4, 4, 256)
    seen, received_2 = after((seen, received_2))
    same = jnp.sum(jnp.where(first_xl, seen[0], seen[1]), 0)
    cross = jnp.sum(jnp.where(first_xl, seen[1], seen[0]), 0)
    row_sum = jnp.concatenate([same[0] + cross[2], same[2] + cross[0]])
    row_over = jnp.concatenate([same[1] + cross[3], same[3] + cross[1]])
    row_prev_two = jnp.concatenate([row_prev, row_prev_other])
    row_next = decay_rate * row_prev_two + (1.0 - decay_rate) * (row_sum / FF + tiny_eps)
    row_own = row_next[:256]

    send_a, far_give, far_keep = terms(where, True, c_1, c_2, w_all, far_core)
    got_a = lax.ppermute(send_a, ("xl", "xh"), DIAG)
    got_far = lax.ppermute(far_give, "xl", SWAP)
    keep_a, own_b, give_b = terms(where, False, c_1, c_2, w_all, near_core)
    got_b = lax.ppermute(give_b, "xl", SWAP)
    last_b = lax.ppermute(far_keep + got_far, ("xl", "xh"), DIAG)
    last_a = lax.ppermute(keep_a[:, 256:] + got_a[:, :256], "xl", SWAP)
    total_a = (keep_a[:, :256] + got_a[:, 256:]) + last_a
    total_b = (own_b + got_b) + last_b
    total = jnp.concatenate([total_a.astype(BF16), total_b.astype(BF16)])

    lane = lax.broadcasted_iota(jnp.int32, (128,), 0)
    pair = jnp.where(lane == 0, jnp.sum(row_over / row_next), jnp.where(lane == 1, jnp.sum(row_next), 0.0))
    totals = jnp.sum(spread(pair, ("y", "z"), 16), 0)
    col_other = lax.ppermute(col_half, "xl", SWAP)
    totals, col_other = after((totals, col_other))
    row_mean = totals[1] / D
    update_rms = jnp.sqrt(row_mean * (totals[0] / (D * FF)))
    scale = jnp.sqrt(row_mean) / jnp.maximum(1.0, update_rms)
    update = clipped(
        where,
        scale,
        1.0 / jnp.sqrt(row_own),
        (g_1, g_2),
        (received_1a, received_1b, received_2[0], received_2[1]),
        1.0 / jnp.sqrt(col_half),
        1.0 / jnp.sqrt(col_other),
    )
    col_next = jnp.where(
        first_xl, jnp.concatenate([col_half, col_other]), jnp.concatenate([col_other, col_half])
    )

    return (total, update, row_own, col_next, update_rms)


def solution(mesh):
    fine = Mesh(mesh.devices.reshape(SIZES), AXES)
    fsdp, mp = ("y", "z", "xl"), ("xh", "c")
    in_specs = (P(fsdp, None), P(fsdp, mp), P(fsdp, mp), P(fsdp), P(mp))
    out_specs = (P(mp, fsdp), P(fsdp, mp), P(fsdp), P(mp), P())
    return jax.shard_map(body, mesh=fine, in_specs=in_specs, out_specs=out_specs, check_vma=False)
```

```python
import jax
import jax.numpy as jnp
from jax import lax
from jax.experimental import pallas as pl
from jax.experimental.pallas import tpu as pltpu
from jax.sharding import Mesh, PartitionSpec as P

D = 8192
FF = 16384
TOKENS = 4096
F32 = jnp.float32
BF16 = jnp.bfloat16

decay_rate = 0.84
tiny_eps = 1e-30

AXES = ("y", "z", "xl", "xh", "c")
SIZES = (4, 4, 2, 2, 2)
SWAP = [(0, 1), (1, 0)]
DIAG = [(0, 3), (3, 0), (1, 2), (2, 1)]
WIDE = 1024
MIB = 1 << 20
TILE = 512
SHORT = pl.CostEstimate(flops=1, bytes_accessed=1, transcendentals=0)
LONG = pl.CostEstimate(flops=2 * 10**10, bytes_accessed=1, transcendentals=0)


def spread(value, axes, count):
    copies = jnp.broadcast_to(value[None], (count,) + value.shape)
    return lax.all_to_all(copies, axes, split_axis=0, concat_axis=0, tiled=True)


def mine(a, n, axis, index):
    return lax.dynamic_slice_in_dim(a, index * n, n, axis)


def shift(a, axis, k):
    return lax.ppermute(a, axis, [(i, (i + k) % 4) for i in range(4)])


def near_three(start, axis):
    return [shift(start, axis, 1), shift(start, axis, 3), shift(start, axis, 2)]


def first_pieces(start, three, then):
    a, b, c = three
    pair = [jnp.concatenate([start, a]), jnp.concatenate([b, c])]
    near = [shift(pair[0], then, 1), shift(pair[1], then, 3)]
    return pair, near, [shift(near[0], then, 1), shift(near[1], then, 3)]


def other_pieces(pair, then):
    return [shift(pair[1], then, 1), shift(pair[0], then, 3)]


PLACES = [
    (a, d)
    for halves, d in (("p", 0), ("q", 0), ("p", 1), ("q", 3), ("p", 2), ("q", 2), ("q", 1), ("p", 3))
    for a in {"p": (0, 1), "q": (3, 2)}[halves]
]


def transposed_tokens(where, mine_first, others, swapped, other_swapped):
    def kernel(where_ref, a_ref, *refs):
        b_refs, c_ref, d_ref, out_ref, hold = refs[:3], *refs[3:]
        xl, xh, c = where_ref[0], where_ref[1], where_ref[2]

        def put(value, xl, xh, c):
            hold[pl.ds(pl.multiple_of(xl * 128 + xh * 64 + c * 32, 32), 32), :] = value

        places = ((xl, xh), (1 - xl, xh), (xl, 1 - xh), (1 - xl, 1 - xh))
        put(a_ref[0], *places[0], c)
        put(c_ref[0], *places[0], 1 - c)
        for k in range(3):
            put(b_refs[k][0], *places[k + 1], c)
            put(d_ref[k, 0], *places[k + 1], 1 - c)
        out_ref[...] = hold[...].T

    block = pl.BlockSpec((1, 32, 512), lambda i, where_ref: (i, 0, 0))
    return pl.pallas_call(
        kernel,
        grid_spec=pltpu.PrefetchScalarGridSpec(
            num_scalar_prefetch=1,
            grid=(16,),
            in_specs=[block] * 5 + [pl.BlockSpec((3, 1, 32, 512), lambda i, where_ref: (0, i, 0, 0))],
            out_specs=pl.BlockSpec((512, 256), lambda i, where_ref: (0, i)),
            scratch_shapes=[pltpu.VMEM((256, 512), BF16)],
        ),
        out_shape=jax.ShapeDtypeStruct((512, TOKENS), BF16),
        cost_estimate=LONG,
    )(where, mine_first, *others, swapped, other_swapped)


def squares_of(g, row_ref, col_ref, columns, first):
    squares = g * g
    rows, width = g.shape
    col_ref[:, columns] = jnp.sum(squares.reshape(rows // 8, 8, width), 0)
    sums = squares[:, :128]
    for k in range(128, width, 128):
        sums = sums + squares[:, k : k + 128]
    if first is True:
        row_ref[...] = sums
    else:
        row_ref[...] += sums


def grad_shapes(width):
    parts = tuple(jax.ShapeDtypeStruct((256, TILE), F32) for _ in range(width // TILE))
    return (
        jax.ShapeDtypeStruct((256, width), F32),
        jax.ShapeDtypeStruct((512, 128), F32),
        jax.ShapeDtypeStruct((8, width), F32),
    ) + parts


def own_other(a, first, axis):
    low, high = (a[:256], a[256:]) if axis == 0 else (a[:, :256], a[:, 256:])
    return jnp.where(first, low, high), jnp.where(first, high, low)


def gradient_of_pieces(xt, pieces, index, xl):
    rows, width = pieces[0].shape
    each = rows // 128
    n = each * len(pieces)

    def kernel(xl_ref, index_ref, xt_ref, *refs):
        ins = refs[: len(pieces)]
        c_ref, own_ref, row_ref, col_ref, *others = refs[len(pieces) : -3]
        hold, in_sems, out_sem = refs[-3:]
        copies = []
        for k in range(n):
            copies.append(
                pltpu.make_async_copy(
                    ins[k // each].at[pl.ds(128 * (k % each), 128)], hold.at[index_ref[k]], in_sems.at[k]
                )
            )
            copies[-1].start()
        for copy in copies:
            copy.wait()
        write = pltpu.make_async_copy(hold, c_ref, out_sem)
        write.start()
        for k, other_ref in enumerate(others):
            columns = slice(k * TILE, (k + 1) * TILE)
            block = hold[:, :, columns].reshape(TOKENS, TILE)
            g = jnp.dot(xt_ref[...], block, preferred_element_type=F32) * float(TOKENS) ** (-0.5)
            own_ref[:, columns], other_ref[...] = own_other(g, xl_ref[0] == 0, 0)
            squares_of(g, row_ref, col_ref, columns, k == 0)
        write.wait()

    vmem = pl.BlockSpec(memory_space=pltpu.VMEM)
    anywhere = pl.BlockSpec(memory_space=pl.ANY)
    smem = pl.BlockSpec(memory_space=pltpu.SMEM)
    out = pl.pallas_call(
        kernel,
        out_shape=(jax.ShapeDtypeStruct((n, 128, width), BF16),) + grad_shapes(width),
        in_specs=[smem, smem, vmem] + [anywhere] * len(pieces),
        out_specs=(anywhere,) + (vmem,) * (3 + width // TILE),
        scratch_shapes=[
            pltpu.VMEM((n, 128, width), BF16),
            pltpu.SemaphoreType.DMA((n,)),
            pltpu.SemaphoreType.DMA,
        ],
        compiler_params=pltpu.CompilerParams(vmem_limit_bytes=56 * MIB),
        cost_estimate=LONG,
    )(xl, index, xt, *pieces)
    return out[0].reshape(TOKENS, width), *out[1:4], out[4:]


def gradient(xt, c_all, xl):
    width = c_all.shape[1]

    def kernel(xl_ref, xt_ref, c_ref, own_ref, row_ref, col_ref, *others):
        g = jnp.dot(xt_ref[...], c_ref[...], preferred_element_type=F32) * float(TOKENS) ** (-0.5)
        own, other = own_other(g, xl_ref[0] == 0, 0)
        own_ref[...] = own
        for k, other_ref in enumerate(others):

            @pl.when(pl.program_id(0) == k)
            def _():
                other_ref[...] = other

        @pl.when(pl.program_id(0) == 0)
        def _():
            row_ref[...] = jnp.zeros_like(row_ref)

        squares_of(g, row_ref, col_ref, slice(None), False)

    out = pl.pallas_call(
        kernel,
        grid=(width // TILE,),
        out_shape=grad_shapes(width),
        in_specs=[
            pl.BlockSpec(memory_space=pltpu.SMEM),
            pl.BlockSpec((512, TOKENS), lambda j: (0, 0)),
            pl.BlockSpec((TOKENS, TILE), lambda j: (0, j)),
        ],
        out_specs=(
            pl.BlockSpec((256, TILE), lambda j: (0, j)),
            pl.BlockSpec((512, 128), lambda j: (0, 0)),
            pl.BlockSpec((8, TILE), lambda j: (0, j)),
        )
        + (pl.BlockSpec((256, TILE), lambda j: (0, 0)),) * (width // TILE),
        compiler_params=pltpu.CompilerParams(vmem_limit_bytes=56 * MIB),
        cost_estimate=LONG,
    )(xl, xt, c_all)
    return *out[:3], out[3:]


def terms(where, far, c_1, c_2, w_all, received=None):
    w1, w2 = c_1.shape[1], c_2.shape[1]
    keep = received is not None

    def kernel(where_ref, c1_ref, c2_ref, w_ref, *refs):
        t = jnp.dot(c1_ref[...], w_ref[:w1], preferred_element_type=F32)
        t = t + jnp.dot(c2_ref[...], w_ref[w1:], preferred_element_type=F32)
        if not keep:
            refs[0][...] = t
            return
        got_ref, both_1, both_2, own, other = refs
        t = t + got_ref[...]

        @pl.when(pl.program_id(0) == 0)
        def _():
            for ref, rows in ((both_1, t[:256]), (both_2, t[256:])):
                ref[:, :256], ref[:, 256:] = own_other(rows, where_ref[0] == 0, 1)

        @pl.when(pl.program_id(0) == 1)
        def _():
            own[...], other[...] = own_other(t, where_ref[0] == 0, 1)

    def rows(i, where_ref):
        high = 1 - where_ref[1] if far else where_ref[1]
        core = where_ref[2] if keep else 1 - where_ref[2]
        return ((2 * high + core) * 2 + i, 0)

    step = pl.BlockSpec((512, 512), lambda i, where_ref: (i, 0))
    block = jax.ShapeDtypeStruct((512, 256), F32)
    whole = [pl.BlockSpec(shape, lambda i, where_ref: (0, 0)) for shape in ((256, 512), (256, 512), (512, 256), (512, 256))]
    return pl.pallas_call(
        kernel,
        grid_spec=pltpu.PrefetchScalarGridSpec(
            num_scalar_prefetch=1,
            grid=(2,),
            in_specs=[
                pl.BlockSpec((512, w1), rows),
                pl.BlockSpec((512, w2), rows),
                pl.BlockSpec((w1 + w2, 512), lambda i, where_ref: (0, 0)),
            ]
            + [step] * keep,
            out_specs=whole if keep else step,
        ),
        out_shape=[jax.ShapeDtypeStruct((256, 512), F32)] * 2 + [block, block]
        if keep
        else jax.ShapeDtypeStruct((1024, 512), F32),
        compiler_params=pltpu.CompilerParams(vmem_limit_bytes=56 * MIB),
        cost_estimate=LONG,
    )(where, c_1, c_2, w_all, *((received,) if keep else ()))


def clipped(where, scale, row_factor, own, received, own_factors, received_factors):
    half = sum(g.shape[1] for g in own)
    tile = half // 2
    blocks = own + received
    firsts = [sum(g.shape[1] for g in blocks[:k]) for k in range(len(blocks))]

    def kernel(where_ref, scale_ref, row_ref, col_ref, *refs):
        out_ref = refs[-1]
        rows = row_ref[...] * scale_ref[0]
        for step in range(4):

            @pl.when(pl.program_id(0) == step)
            def _():
                for ref, first in zip(refs, firsts):
                    low, high = max(first, step * tile), min(first + ref.shape[1], (step + 1) * tile)
                    if low < high:
                        to = slice(low - step * tile, high - step * tile)
                        out_ref[:, to] = ref[:, low - first : high - first] * rows * col_ref[:, to]

    def place(j, where_ref):
        own_half = where_ref[0] + (j // 2) * (1 - 2 * where_ref[0])
        return (0, own_half * 2 + j % 2)

    return pl.pallas_call(
        kernel,
        grid_spec=pltpu.PrefetchScalarGridSpec(
            num_scalar_prefetch=1,
            grid=(4,),
            in_specs=[
                pl.BlockSpec(memory_space=pltpu.SMEM),
                pl.BlockSpec((256, 1), lambda j, where_ref: (0, 0)),
                pl.BlockSpec((1, tile), lambda j, where_ref: (0, j)),
            ]
            + [pl.BlockSpec(g.shape, lambda j, where_ref: (0, 0)) for g in blocks],
            out_specs=pl.BlockSpec((256, tile), place),
        ),
        out_shape=jax.ShapeDtypeStruct((256, 2 * half), F32),
        compiler_params=pltpu.CompilerParams(vmem_limit_bytes=56 * MIB),
        cost_estimate=LONG,
    )(
        where,
        scale.reshape(1),
        row_factor[:, None],
        jnp.concatenate([own_factors, received_factors])[None, :],
        *blocks,
    )


def body(tokens, cotangent, weight, row_prev, col_prev):
    y, z = lax.axis_index("y"), lax.axis_index("z")
    xl, xh, c = lax.axis_index("xl"), lax.axis_index("xh"), lax.axis_index("c")
    half = cotangent.shape[1] // 2
    first_xl = xl == 0
    after = lax.optimization_barrier

    where = jnp.stack([xl, xh, c]).astype(jnp.int32)

    away = mine(cotangent, half, 1, 1 - xl)
    part, away = after((mine(tokens, 32, 0, 2 * xh + c), away))
    other = lax.ppermute(away, "xl", SWAP)
    part = part.reshape(32, 16, 512)
    xo = lax.all_to_all(part, ("y", "z"), split_axis=1, concat_axis=0, tiled=False)

    own = mine(cotangent, half, 1, xl)
    row_prev_other = lax.ppermute(row_prev, "xl", SWAP)
    own, other, xo, row_prev_other = after((own, other, xo, row_prev_other))
    own_1, own_2 = own[:, :WIDE], own[:, WIDE:]
    other_1, other_2 = other[:, :WIDE], other[:, WIDE:]
    shard = jnp.where(first_xl, jnp.stack([own_2, other_2]), jnp.stack([other_2, own_2]))
    c_2 = lax.all_gather(shard, ("y", "z"), axis=0, tiled=False).reshape(TOKENS, half - WIDE)
    pair, near, far = first_pieces(own_1, near_three(own_1, "y"), "z")
    pair_2, near_2, far_2 = first_pieces(other_1, near_three(other_1, "z"), "y")

    to = lax.ppermute(xo, "c", SWAP)
    xs = [lax.ppermute(xo, "xl", SWAP), lax.ppermute(xo, "xh", SWAP), lax.ppermute(xo, ("xl", "xh"), DIAG)]
    xs, near, near_2 = after((xs, near, near_2))
    xt = transposed_tokens(where, xo, xs, to, lax.ppermute(jnp.stack(xs), "c", SWAP))
    pair, pair_2, xt = after((pair, pair_2, xt))
    pieces = pair + near + far + other_pieces(pair, "z") + pair_2 + near_2 + far_2 + other_pieces(pair_2, "y")
    index = [((y - dy) % 4 * 4 + (z - dz) % 4) * 2 + xl for dy, dz in PLACES]
    index += [((y - dy) % 4 * 4 + (z - dz) % 4) * 2 + 1 - xl for dz, dy in PLACES]
    w_own = mine(weight, half, 1, xl)
    w_other = lax.ppermute(mine(weight, half, 1, 1 - xl), "xl", SWAP)
    w_other, xt = after((w_other, xt))
    w_all = jnp.where(first_xl, jnp.concatenate([w_own, w_other]), jnp.concatenate([w_other, w_own])).T

    g_2, rows_2, cols_2, send_2 = gradient(xt, c_2, where)
    received_2 = [lax.ppermute(g, "xl", SWAP) for g in send_2]
    pieces, w_all, xt, rows_2 = after((pieces, w_all, xt, rows_2))
    c_1, g_1, rows_1, cols_1, send_1 = gradient_of_pieces(xt, pieces, jnp.stack(index).astype(jnp.int32), where)
    received_1 = [lax.ppermute(g, "xl", SWAP) for g in send_1]
    cols = jnp.sum(jnp.concatenate([cols_1, cols_2], 1), 0)
    w_all, received_2[0], cols = after((w_all, received_2[0], cols))
    col_sum = jnp.sum(spread(cols, ("y", "z"), 16), 0)
    far_terms = terms(where, True, c_1, c_2, w_all)
    far_core = lax.ppermute(far_terms, "c", SWAP)
    far_terms, received_1[0], col_sum, w_all = after((far_terms, received_1[0], col_sum, w_all))

    col_prev_mine = mine(col_prev, half, 0, xl)
    col_half = decay_rate * col_prev_mine + (1.0 - decay_rate) * (col_sum / D + tiny_eps)
    near_terms = terms(where, False, c_1, c_2, w_all)
    near_core = lax.ppermute(near_terms, "c", SWAP)
    near_terms, far_core, received_1[1] = after((near_terms, far_core, received_1[1]))

    def over_columns(g, col):
        return jnp.sum(g * g * (1.0 / col)[None, :], 1)

    col_1, col_2 = col_half[:WIDE], col_half[WIDE:]
    over_own = over_columns(g_1, col_1) + over_columns(g_2, col_2)
    over_other, first = 0.0, 0
    for g in send_1 + send_2:
        over_other = over_other + over_columns(g, col_half[first : first + g.shape[1]])
        first += g.shape[1]
    plain = jnp.sum(rows_1 + rows_2, 1)
    plain_own, plain_other = own_other(plain, first_xl, 0)
    sums = jnp.stack([plain_own, over_own, plain_other, over_other])
    give_1, give_2, far_give, far_keep = terms(where, True, c_1, c_2, w_all, far_core)
    seen = spread(sums, ("xl", "xh", "c"), 8).reshape(2, 4, 4, 256)
    got_1 = lax.ppermute(give_1, ("xl", "xh"), DIAG)
    got_far = lax.ppermute(far_give, "xl", SWAP)
    keep_1, keep_2, own_b, give_b = terms(where, False, c_1, c_2, w_all, near_core)
    seen, far_keep, received_2[1], got_1, got_far, keep_1, give_b = after(
        (seen, far_keep, received_2[1], got_1, got_far, keep_1, give_b)
    )
    same = jnp.sum(jnp.where(first_xl, seen[0], seen[1]), 0)
    cross = jnp.sum(jnp.where(first_xl, seen[1], seen[0]), 0)
    row_sum = jnp.concatenate([same[0] + cross[2], same[2] + cross[0]])
    row_over = jnp.concatenate([same[1] + cross[3], same[3] + cross[1]])
    row_prev_two = jnp.concatenate([row_prev, row_prev_other])
    row_next = decay_rate * row_prev_two + (1.0 - decay_rate) * (row_sum / FF + tiny_eps)
    row_own = row_next[:256]

    lane = lax.broadcasted_iota(jnp.int32, (128,), 0)
    pair = jnp.where(lane == 0, jnp.sum(row_over / row_next), jnp.where(lane == 1, jnp.sum(row_next), 0.0))
    totals = spread(pair, ("y", "z"), 16)
    got_2 = lax.ppermute(give_2, ("xl", "xh"), DIAG)
    col_other = lax.ppermute(col_half, "xl", SWAP)
    got_b = lax.ppermute(give_b, "xl", SWAP)
    totals, col_other, got_2, got_b = after((totals, col_other, got_2, got_b))
    totals = jnp.sum(totals, 0)
    last_b = lax.ppermute(far_keep + got_far, ("xl", "xh"), DIAG)
    keep_a, got_a = jnp.concatenate([keep_1, keep_2]), jnp.concatenate([got_1, got_2])
    last_a = lax.ppermute(keep_a[:, 256:] + got_a[:, :256], "xl", SWAP)
    row_mean = totals[1] / D
    update_rms = jnp.sqrt(row_mean * (totals[0] / (D * FF)))
    scale = jnp.sqrt(row_mean) / jnp.maximum(1.0, update_rms)
    update = clipped(
        where,
        scale,
        1.0 / jnp.sqrt(row_own),
        (g_1, g_2),
        (*received_1, *received_2),
        1.0 / jnp.sqrt(col_half),
        1.0 / jnp.sqrt(col_other),
    )
    col_next = jnp.where(
        first_xl, jnp.concatenate([col_half, col_other]), jnp.concatenate([col_other, col_half])
    )

    total_a = (keep_a[:, :256] + got_a[:, 256:]) + last_a
    total_b = (own_b + got_b) + last_b
    total = jnp.concatenate([total_a.astype(BF16), total_b.astype(BF16)])

    return (total, update, row_own, col_next, update_rms)


def solution(mesh):
    fine = Mesh(mesh.devices.reshape(SIZES), AXES)
    fsdp, mp = ("y", "z", "xl"), ("xh", "c")
    in_specs = (P(fsdp, None), P(fsdp, mp), P(fsdp, mp), P(fsdp), P(mp))
    out_specs = (P(mp, fsdp), P(fsdp, mp), P(fsdp), P(mp), P())
    return jax.shard_map(body, mesh=fine, in_specs=in_specs, out_specs=out_specs, check_vma=False)
```

```python
import jax
import jax.numpy as jnp
from jax import lax
from jax.experimental import pallas as pl
from jax.experimental.pallas import tpu as pltpu
from jax.sharding import Mesh, PartitionSpec as P

D = 8192
FF = 16384
TOKENS = 4096
F32 = jnp.float32
BF16 = jnp.bfloat16

decay_rate = 0.84
tiny_eps = 1e-30

AXES = ("y", "z", "xl", "xh", "c")
SIZES = (4, 4, 2, 2, 2)
SWAP = [(0, 1), (1, 0)]
DIAG = [(0, 3), (3, 0), (1, 2), (2, 1)]
WIDE = 1024
MIB = 1 << 20
TILE = 512
SHORT = pl.CostEstimate(flops=1, bytes_accessed=1, transcendentals=0)
LONG = pl.CostEstimate(flops=2 * 10**10, bytes_accessed=1, transcendentals=0)


def spread(value, axes, count):
    copies = jnp.broadcast_to(value[None], (count,) + value.shape)
    return lax.all_to_all(copies, axes, split_axis=0, concat_axis=0, tiled=True)


def mine(a, n, axis, index):
    return lax.dynamic_slice_in_dim(a, index * n, n, axis)


def shift(a, axis, k):
    return lax.ppermute(a, axis, [(i, (i + k) % 4) for i in range(4)])


def near_three(start, axis):
    return [shift(start, axis, 1), shift(start, axis, 3), shift(start, axis, 2)]


def first_pieces(start, three, then):
    a, b, c = three
    pair = [jnp.concatenate([start, a]), jnp.concatenate([b, c])]
    near = [shift(pair[0], then, 1), shift(pair[1], then, 3)]
    return pair, near, [shift(near[0], then, 1), shift(near[1], then, 3)]


def other_pieces(pair, then):
    return [shift(pair[1], then, 1), shift(pair[0], then, 3)]


PLACES = [
    (a, d)
    for halves, d in (("p", 0), ("q", 0), ("p", 1), ("q", 3), ("p", 2), ("q", 2), ("q", 1), ("p", 3))
    for a in {"p": (0, 1), "q": (3, 2)}[halves]
]


def transposed_tokens(where, mine_first, others, swapped, other_swapped):
    def kernel(where_ref, a_ref, *refs):
        b_refs, c_ref, d_ref, out_ref, hold = refs[:3], *refs[3:]
        xl, xh, c = where_ref[0], where_ref[1], where_ref[2]

        def put(value, xl, xh, c):
            hold[pl.ds(pl.multiple_of(xl * 128 + xh * 64 + c * 32, 32), 32), :] = value

        places = ((xl, xh), (1 - xl, xh), (xl, 1 - xh), (1 - xl, 1 - xh))
        put(a_ref[0], *places[0], c)
        put(c_ref[0], *places[0], 1 - c)
        for k in range(3):
            put(b_refs[k][0], *places[k + 1], c)
            put(d_ref[k, 0], *places[k + 1], 1 - c)
        out_ref[...] = hold[...].T

    block = pl.BlockSpec((1, 32, 512), lambda i, where_ref: (i, 0, 0))
    return pl.pallas_call(
        kernel,
        grid_spec=pltpu.PrefetchScalarGridSpec(
            num_scalar_prefetch=1,
            grid=(16,),
            in_specs=[block] * 5 + [pl.BlockSpec((3, 1, 32, 512), lambda i, where_ref: (0, i, 0, 0))],
            out_specs=pl.BlockSpec((512, 256), lambda i, where_ref: (0, i)),
            scratch_shapes=[pltpu.VMEM((256, 512), BF16)],
        ),
        out_shape=jax.ShapeDtypeStruct((512, TOKENS), BF16),
        cost_estimate=LONG,
    )(where, mine_first, *others, swapped, other_swapped)


def squares_of(g, row_ref, col_ref, columns, first):
    squares = g * g
    rows, width = g.shape
    col_ref[:, columns] = jnp.sum(squares.reshape(rows // 8, 8, width), 0)
    sums = squares[:, :128]
    for k in range(128, width, 128):
        sums = sums + squares[:, k : k + 128]
    if first is True:
        row_ref[...] = sums
    else:
        row_ref[...] += sums


def grad_shapes(width):
    parts = tuple(jax.ShapeDtypeStruct((256, TILE), F32) for _ in range(width // TILE))
    return (
        jax.ShapeDtypeStruct((256, width), F32),
        jax.ShapeDtypeStruct((512, 128), F32),
        jax.ShapeDtypeStruct((8, width), F32),
    ) + parts


def own_other(a, first, axis):
    low, high = (a[:256], a[256:]) if axis == 0 else (a[:, :256], a[:, 256:])
    return jnp.where(first, low, high), jnp.where(first, high, low)


def gradient_of_pieces(xt, pieces, index, xl):
    rows, width = pieces[0].shape
    each = rows // 128
    n = each * len(pieces)

    def kernel(xl_ref, index_ref, xt_ref, *refs):
        ins = refs[: len(pieces)]
        c_ref, own_ref, row_ref, col_ref, *others = refs[len(pieces) : -3]
        hold, in_sems, out_sem = refs[-3:]
        copies = []
        for k in range(n):
            copies.append(
                pltpu.make_async_copy(
                    ins[k // each].at[pl.ds(128 * (k % each), 128)], hold.at[index_ref[k]], in_sems.at[k]
                )
            )
            copies[-1].start()
        for copy in copies:
            copy.wait()
        write = pltpu.make_async_copy(hold, c_ref, out_sem)
        write.start()
        for k, other_ref in enumerate(others):
            columns = slice(k * TILE, (k + 1) * TILE)
            block = hold[:, :, columns].reshape(TOKENS, TILE)
            g = jnp.dot(xt_ref[...], block, preferred_element_type=F32) * float(TOKENS) ** (-0.5)
            own_ref[:, columns], other_ref[...] = own_other(g, xl_ref[0] == 0, 0)
            squares_of(g, row_ref, col_ref, columns, k == 0)
        write.wait()

    vmem = pl.BlockSpec(memory_space=pltpu.VMEM)
    anywhere = pl.BlockSpec(memory_space=pl.ANY)
    smem = pl.BlockSpec(memory_space=pltpu.SMEM)
    out = pl.pallas_call(
        kernel,
        out_shape=(jax.ShapeDtypeStruct((n, 128, width), BF16),) + grad_shapes(width),
        in_specs=[smem, smem, vmem] + [anywhere] * len(pieces),
        out_specs=(anywhere,) + (vmem,) * (3 + width // TILE),
        scratch_shapes=[
            pltpu.VMEM((n, 128, width), BF16),
            pltpu.SemaphoreType.DMA((n,)),
            pltpu.SemaphoreType.DMA,
        ],
        compiler_params=pltpu.CompilerParams(vmem_limit_bytes=56 * MIB),
        cost_estimate=LONG,
    )(xl, index, xt, *pieces)
    return out[0].reshape(TOKENS, width), *out[1:4], out[4:]


def gradient(xt, c_all, xl):
    width = c_all.shape[1]

    def kernel(xl_ref, xt_ref, c_ref, own_ref, row_ref, col_ref, *others):
        g = jnp.dot(xt_ref[...], c_ref[...], preferred_element_type=F32) * float(TOKENS) ** (-0.5)
        own, other = own_other(g, xl_ref[0] == 0, 0)
        own_ref[...] = own
        for k, other_ref in enumerate(others):

            @pl.when(pl.program_id(0) == k)
            def _():
                other_ref[...] = other

        @pl.when(pl.program_id(0) == 0)
        def _():
            row_ref[...] = jnp.zeros_like(row_ref)

        squares_of(g, row_ref, col_ref, slice(None), False)

    out = pl.pallas_call(
        kernel,
        grid=(width // TILE,),
        out_shape=grad_shapes(width),
        in_specs=[
            pl.BlockSpec(memory_space=pltpu.SMEM),
            pl.BlockSpec((512, TOKENS), lambda j: (0, 0)),
            pl.BlockSpec((TOKENS, TILE), lambda j: (0, j)),
        ],
        out_specs=(
            pl.BlockSpec((256, TILE), lambda j: (0, j)),
            pl.BlockSpec((512, 128), lambda j: (0, 0)),
            pl.BlockSpec((8, TILE), lambda j: (0, j)),
        )
        + (pl.BlockSpec((256, TILE), lambda j: (0, 0)),) * (width // TILE),
        compiler_params=pltpu.CompilerParams(vmem_limit_bytes=56 * MIB),
        cost_estimate=LONG,
    )(xl, xt, c_all)
    return *out[:3], out[3:]


def terms(where, far, c_1, c_2, w_all, received=None):
    w1, w2 = c_1.shape[1], c_2.shape[1]
    keep = received is not None

    def kernel(where_ref, c1_ref, c2_ref, w_ref, *refs):
        t = jnp.dot(c1_ref[...], w_ref[:w1], preferred_element_type=F32)
        t = t + jnp.dot(c2_ref[...], w_ref[w1:], preferred_element_type=F32)
        if not keep:
            refs[0][...] = t
            return
        got_ref, both_1, both_2, own, other = refs
        t = t + got_ref[...]

        @pl.when(pl.program_id(0) == 0)
        def _():
            for ref, rows in ((both_1, t[:256]), (both_2, t[256:])):
                ref[:, :256], ref[:, 256:] = own_other(rows, where_ref[0] == 0, 1)

        @pl.when(pl.program_id(0) == 1)
        def _():
            own[...], other[...] = own_other(t, where_ref[0] == 0, 1)

    def rows(i, where_ref):
        high = 1 - where_ref[1] if far else where_ref[1]
        core = where_ref[2] if keep else 1 - where_ref[2]
        return ((2 * high + core) * 2 + i, 0)

    step = pl.BlockSpec((512, 512), lambda i, where_ref: (i, 0))
    block = jax.ShapeDtypeStruct((512, 256), F32)
    whole = [pl.BlockSpec(shape, lambda i, where_ref: (0, 0)) for shape in ((256, 512), (256, 512), (512, 256), (512, 256))]
    return pl.pallas_call(
        kernel,
        grid_spec=pltpu.PrefetchScalarGridSpec(
            num_scalar_prefetch=1,
            grid=(2,),
            in_specs=[
                pl.BlockSpec((512, w1), rows),
                pl.BlockSpec((512, w2), rows),
                pl.BlockSpec((w1 + w2, 512), lambda i, where_ref: (0, 0)),
            ]
            + [step] * keep,
            out_specs=whole if keep else step,
        ),
        out_shape=[jax.ShapeDtypeStruct((256, 512), F32)] * 2 + [block, block]
        if keep
        else jax.ShapeDtypeStruct((1024, 512), F32),
        compiler_params=pltpu.CompilerParams(vmem_limit_bytes=56 * MIB),
        cost_estimate=LONG,
    )(where, c_1, c_2, w_all, *((received,) if keep else ()))


def clipped(where, scale, row_factor, own, received, own_factors, received_factors):
    half = sum(g.shape[1] for g in own)
    tile = half // 2
    blocks = own + received
    firsts = [sum(g.shape[1] for g in blocks[:k]) for k in range(len(blocks))]

    def kernel(where_ref, scale_ref, row_ref, col_ref, *refs):
        out_ref = refs[-1]
        rows = row_ref[...] * scale_ref[0]
        for step in range(4):

            @pl.when(pl.program_id(0) == step)
            def _():
                for ref, first in zip(refs, firsts):
                    low, high = max(first, step * tile), min(first + ref.shape[1], (step + 1) * tile)
                    if low < high:
                        to = slice(low - step * tile, high - step * tile)
                        out_ref[:, to] = ref[:, low - first : high - first] * rows * col_ref[:, to]

    def place(j, where_ref):
        own_half = where_ref[0] + (j // 2) * (1 - 2 * where_ref[0])
        return (0, own_half * 2 + j % 2)

    return pl.pallas_call(
        kernel,
        grid_spec=pltpu.PrefetchScalarGridSpec(
            num_scalar_prefetch=1,
            grid=(4,),
            in_specs=[
                pl.BlockSpec(memory_space=pltpu.SMEM),
                pl.BlockSpec((256, 1), lambda j, where_ref: (0, 0)),
                pl.BlockSpec((1, tile), lambda j, where_ref: (0, j)),
            ]
            + [pl.BlockSpec(g.shape, lambda j, where_ref: (0, 0)) for g in blocks],
            out_specs=pl.BlockSpec((256, tile), place),
        ),
        out_shape=jax.ShapeDtypeStruct((256, 2 * half), F32),
        compiler_params=pltpu.CompilerParams(vmem_limit_bytes=56 * MIB),
        cost_estimate=LONG,
    )(
        where,
        scale.reshape(1),
        row_factor[:, None],
        jnp.concatenate([own_factors, received_factors])[None, :],
        *blocks,
    )


def body(tokens, cotangent, weight, row_prev, col_prev):
    y, z = lax.axis_index("y"), lax.axis_index("z")
    xl, xh, c = lax.axis_index("xl"), lax.axis_index("xh"), lax.axis_index("c")
    half = cotangent.shape[1] // 2
    first_xl = xl == 0
    after = lax.optimization_barrier

    where = jnp.stack([xl, xh, c]).astype(jnp.int32)

    away = mine(cotangent, half, 1, 1 - xl)
    part, away = after((mine(tokens, 32, 0, 2 * xh + c), away))
    other = lax.ppermute(away, "xl", SWAP)
    part = part.reshape(32, 16, 512)
    xo = lax.all_to_all(part, ("y", "z"), split_axis=1, concat_axis=0, tiled=False)

    own = mine(cotangent, half, 1, xl)
    row_prev_other = lax.ppermute(row_prev, "xl", SWAP)
    own, other, xo, row_prev_other = after((own, other, xo, row_prev_other))
    own_1, own_2 = own[:, :WIDE], own[:, WIDE:]
    other_1, other_2 = other[:, :WIDE], other[:, WIDE:]
    shard = jnp.where(first_xl, jnp.stack([own_2, other_2]), jnp.stack([other_2, own_2]))
    c_2 = lax.all_gather(shard, ("y", "z"), axis=0, tiled=False).reshape(TOKENS, half - WIDE)
    pair, near, far = first_pieces(own_1, near_three(own_1, "y"), "z")
    pair_2, near_2, far_2 = first_pieces(other_1, near_three(other_1, "z"), "y")

    to = lax.ppermute(xo, "c", SWAP)
    xs = [lax.ppermute(xo, "xl", SWAP), lax.ppermute(xo, "xh", SWAP), lax.ppermute(xo, ("xl", "xh"), DIAG)]
    xs, near, near_2 = after((xs, near, near_2))
    xt = transposed_tokens(where, xo, xs, to, lax.ppermute(jnp.stack(xs), "c", SWAP))
    pair, pair_2, xt = after((pair, pair_2, xt))
    pieces = pair + near + far + other_pieces(pair, "z") + pair_2 + near_2 + far_2 + other_pieces(pair_2, "y")
    index = [((y - dy) % 4 * 4 + (z - dz) % 4) * 2 + xl for dy, dz in PLACES]
    index += [((y - dy) % 4 * 4 + (z - dz) % 4) * 2 + 1 - xl for dz, dy in PLACES]
    w_own = mine(weight, half, 1, xl)
    w_other = lax.ppermute(mine(weight, half, 1, 1 - xl), "xl", SWAP)
    w_other, xt = after((w_other, xt))
    w_all = jnp.where(first_xl, jnp.concatenate([w_own, w_other]), jnp.concatenate([w_other, w_own])).T

    g_2, rows_2, cols_2, send_2 = gradient(xt, c_2, where)
    received_2 = [lax.ppermute(g, "xl", SWAP) for g in send_2]
    pieces, w_all, xt, rows_2 = after((pieces, w_all, xt, rows_2))
    c_1, g_1, rows_1, cols_1, send_1 = gradient_of_pieces(xt, pieces, jnp.stack(index).astype(jnp.int32), where)
    received_1 = [lax.ppermute(g, "xl", SWAP) for g in send_1]
    cols = jnp.sum(jnp.concatenate([cols_1, cols_2], 1), 0)
    w_all, received_2[0], cols = after((w_all, received_2[0], cols))
    col_sum = jnp.sum(spread(cols, ("y", "z"), 16), 0)
    far_terms = terms(where, True, c_1, c_2, w_all)
    far_core = lax.ppermute(far_terms, "c", SWAP)
    far_terms, received_1[0], col_sum, w_all = after((far_terms, received_1[0], col_sum, w_all))

    col_prev_mine = mine(col_prev, half, 0, xl)
    col_half = decay_rate * col_prev_mine + (1.0 - decay_rate) * (col_sum / D + tiny_eps)
    near_terms = terms(where, False, c_1, c_2, w_all)
    near_core = lax.ppermute(near_terms, "c", SWAP)
    near_terms, far_core, received_1[1] = after((near_terms, far_core, received_1[1]))

    def over_columns(g, col):
        return jnp.sum(g * g * (1.0 / col)[None, :], 1)

    col_1, col_2 = col_half[:WIDE], col_half[WIDE:]
    over_own = over_columns(g_1, col_1) + over_columns(g_2, col_2)
    over_other, first = 0.0, 0
    for g in send_1 + send_2:
        over_other = over_other + over_columns(g, col_half[first : first + g.shape[1]])
        first += g.shape[1]
    plain = jnp.sum(rows_1 + rows_2, 1)
    plain_own, plain_other = own_other(plain, first_xl, 0)
    sums = jnp.stack([plain_own, over_own, plain_other, over_other])
    give_1, give_2, far_give, far_keep = terms(where, True, c_1, c_2, w_all, far_core)
    seen = spread(sums, ("xl", "xh", "c"), 8).reshape(2, 4, 4, 256)
    got_1 = lax.ppermute(give_1, ("xl", "xh"), DIAG)
    got_far = lax.ppermute(far_give, "xl", SWAP)
    keep_1, keep_2, own_b, give_b = terms(where, False, c_1, c_2, w_all, near_core)
    seen, far_keep, received_2[1], keep_1, give_b = after((seen, far_keep, received_2[1], keep_1, give_b))
    same = jnp.sum(jnp.where(first_xl, seen[0], seen[1]), 0)
    cross = jnp.sum(jnp.where(first_xl, seen[1], seen[0]), 0)
    row_sum = jnp.concatenate([same[0] + cross[2], same[2] + cross[0]])
    row_over = jnp.concatenate([same[1] + cross[3], same[3] + cross[1]])
    row_prev_two = jnp.concatenate([row_prev, row_prev_other])
    row_next = decay_rate * row_prev_two + (1.0 - decay_rate) * (row_sum / FF + tiny_eps)
    row_own = row_next[:256]

    lane = lax.broadcasted_iota(jnp.int32, (128,), 0)
    pair = jnp.where(lane == 0, jnp.sum(row_over / row_next), jnp.where(lane == 1, jnp.sum(row_next), 0.0))
    totals = spread(pair, ("y", "z"), 16)
    got_2 = lax.ppermute(give_2, ("xl", "xh"), DIAG)
    col_other = lax.ppermute(col_half, "xl", SWAP)
    got_b = lax.ppermute(give_b, "xl", SWAP)
    totals, col_other, got_1, got_far, got_2, got_b = after((totals, col_other, got_1, got_far, got_2, got_b))
    totals = jnp.sum(totals, 0)
    last_b = lax.ppermute(far_keep + got_far, ("xl", "xh"), DIAG)
    keep_a, got_a = jnp.concatenate([keep_1, keep_2]), jnp.concatenate([got_1, got_2])
    last_a = lax.ppermute(keep_a[:, 256:] + got_a[:, :256], "xl", SWAP)
    row_mean = totals[1] / D
    update_rms = jnp.sqrt(row_mean * (totals[0] / (D * FF)))
    scale = jnp.sqrt(row_mean) / jnp.maximum(1.0, update_rms)
    update = clipped(
        where,
        scale,
        1.0 / jnp.sqrt(row_own),
        (g_1, g_2),
        (*received_1, *received_2),
        1.0 / jnp.sqrt(col_half),
        1.0 / jnp.sqrt(col_other),
    )
    col_next = jnp.where(
        first_xl, jnp.concatenate([col_half, col_other]), jnp.concatenate([col_other, col_half])
    )

    total_a = (keep_a[:, :256] + got_a[:, 256:]) + last_a
    total_b = (own_b + got_b) + last_b
    total = jnp.concatenate([total_a.astype(BF16), total_b.astype(BF16)])

    return (total, update, row_own, col_next, update_rms)


def solution(mesh):
    fine = Mesh(mesh.devices.reshape(SIZES), AXES)
    fsdp, mp = ("y", "z", "xl"), ("xh", "c")
    in_specs = (P(fsdp, None), P(fsdp, mp), P(fsdp, mp), P(fsdp), P(mp))
    out_specs = (P(mp, fsdp), P(fsdp, mp), P(fsdp), P(mp), P())
    return jax.shard_map(body, mesh=fine, in_specs=in_specs, out_specs=out_specs, check_vma=False)
```

```python
import jax
import jax.numpy as jnp
from jax import lax
from jax.experimental import pallas as pl
from jax.experimental.pallas import tpu as pltpu
from jax.sharding import Mesh, PartitionSpec as P

D = 8192
FF = 16384
TOKENS = 4096
F32 = jnp.float32
BF16 = jnp.bfloat16

decay_rate = 0.84
tiny_eps = 1e-30

AXES = ("y", "z", "xl", "xh", "c")
SIZES = (4, 4, 2, 2, 2)
SWAP = [(0, 1), (1, 0)]
DIAG = [(0, 3), (3, 0), (1, 2), (2, 1)]
WIDE = 1024
MIB = 1 << 20
TILE = 512
SHORT = pl.CostEstimate(flops=1, bytes_accessed=1, transcendentals=0)
LONG = pl.CostEstimate(flops=2 * 10**10, bytes_accessed=1, transcendentals=0)


def spread(value, axes, count):
    copies = jnp.broadcast_to(value[None], (count,) + value.shape)
    return lax.all_to_all(copies, axes, split_axis=0, concat_axis=0, tiled=True)


def mine(a, n, axis, index):
    return lax.dynamic_slice_in_dim(a, index * n, n, axis)


def shift(a, axis, k):
    return lax.ppermute(a, axis, [(i, (i + k) % 4) for i in range(4)])


def near_three(start, axis):
    return [shift(start, axis, 1), shift(start, axis, 3), shift(start, axis, 2)]


def first_pieces(start, three, then):
    a, b, c = three
    pair = [jnp.concatenate([start, a]), jnp.concatenate([b, c])]
    near = [shift(pair[0], then, 1), shift(pair[1], then, 3)]
    return pair, near, [shift(near[0], then, 1), shift(near[1], then, 3)]


def other_pieces(pair, then):
    return [shift(pair[1], then, 1), shift(pair[0], then, 3)]


PLACES = [
    (a, d)
    for halves, d in (("p", 0), ("q", 0), ("p", 1), ("q", 3), ("p", 2), ("q", 2), ("q", 1), ("p", 3))
    for a in {"p": (0, 1), "q": (3, 2)}[halves]
]


def transposed_tokens(where, mine_first, others, swapped, other_swapped):
    def kernel(where_ref, a_ref, *refs):
        b_refs, c_ref, d_ref, out_ref, hold = refs[:3], *refs[3:]
        xl, xh, c = where_ref[0], where_ref[1], where_ref[2]

        def put(value, xl, xh, c):
            hold[pl.ds(pl.multiple_of(xl * 128 + xh * 64 + c * 32, 32), 32), :] = value

        places = ((xl, xh), (1 - xl, xh), (xl, 1 - xh), (1 - xl, 1 - xh))
        put(a_ref[0], *places[0], c)
        put(c_ref[0], *places[0], 1 - c)
        for k in range(3):
            put(b_refs[k][0], *places[k + 1], c)
            put(d_ref[k, 0], *places[k + 1], 1 - c)
        out_ref[...] = hold[...].T

    block = pl.BlockSpec((1, 32, 512), lambda i, where_ref: (i, 0, 0))
    return pl.pallas_call(
        kernel,
        grid_spec=pltpu.PrefetchScalarGridSpec(
            num_scalar_prefetch=1,
            grid=(16,),
            in_specs=[block] * 5 + [pl.BlockSpec((3, 1, 32, 512), lambda i, where_ref: (0, i, 0, 0))],
            out_specs=pl.BlockSpec((512, 256), lambda i, where_ref: (0, i)),
            scratch_shapes=[pltpu.VMEM((256, 512), BF16)],
        ),
        out_shape=jax.ShapeDtypeStruct((512, TOKENS), BF16),
        cost_estimate=LONG,
    )(where, mine_first, *others, swapped, other_swapped)


def squares_of(g, row_ref, col_ref, columns, first):
    squares = g * g
    rows, width = g.shape
    col_ref[:, columns] = jnp.sum(squares.reshape(rows // 8, 8, width), 0)
    sums = squares[:, :128]
    for k in range(128, width, 128):
        sums = sums + squares[:, k : k + 128]
    if first is True:
        row_ref[...] = sums
    else:
        row_ref[...] += sums


def grad_shapes(width):
    parts = tuple(jax.ShapeDtypeStruct((256, TILE), F32) for _ in range(width // TILE))
    return (
        jax.ShapeDtypeStruct((256, width), F32),
        jax.ShapeDtypeStruct((512, 128), F32),
        jax.ShapeDtypeStruct((8, width), F32),
    ) + parts


def own_other(a, first, axis):
    low, high = (a[:256], a[256:]) if axis == 0 else (a[:, :256], a[:, 256:])
    return jnp.where(first, low, high), jnp.where(first, high, low)


def gradient_of_pieces(xt, pieces, index, xl):
    rows, width = pieces[0].shape
    each = rows // 128
    n = each * len(pieces)

    def kernel(xl_ref, index_ref, xt_ref, *refs):
        ins = refs[: len(pieces)]
        c_ref, own_ref, row_ref, col_ref, *others = refs[len(pieces) : -3]
        hold, in_sems, out_sem = refs[-3:]
        copies = []
        for k in range(n):
            copies.append(
                pltpu.make_async_copy(
                    ins[k // each].at[pl.ds(128 * (k % each), 128)], hold.at[index_ref[k]], in_sems.at[k]
                )
            )
            copies[-1].start()
        for copy in copies:
            copy.wait()
        write = pltpu.make_async_copy(hold, c_ref, out_sem)
        write.start()
        for k, other_ref in enumerate(others):
            columns = slice(k * TILE, (k + 1) * TILE)
            block = hold[:, :, columns].reshape(TOKENS, TILE)
            g = jnp.dot(xt_ref[...], block, preferred_element_type=F32) * float(TOKENS) ** (-0.5)
            own_ref[:, columns], other_ref[...] = own_other(g, xl_ref[0] == 0, 0)
            squares_of(g, row_ref, col_ref, columns, k == 0)
        write.wait()

    vmem = pl.BlockSpec(memory_space=pltpu.VMEM)
    anywhere = pl.BlockSpec(memory_space=pl.ANY)
    smem = pl.BlockSpec(memory_space=pltpu.SMEM)
    out = pl.pallas_call(
        kernel,
        out_shape=(jax.ShapeDtypeStruct((n, 128, width), BF16),) + grad_shapes(width),
        in_specs=[smem, smem, vmem] + [anywhere] * len(pieces),
        out_specs=(anywhere,) + (vmem,) * (3 + width // TILE),
        scratch_shapes=[
            pltpu.VMEM((n, 128, width), BF16),
            pltpu.SemaphoreType.DMA((n,)),
            pltpu.SemaphoreType.DMA,
        ],
        compiler_params=pltpu.CompilerParams(vmem_limit_bytes=56 * MIB),
        cost_estimate=LONG,
    )(xl, index, xt, *pieces)
    return out[0].reshape(TOKENS, width), *out[1:4], out[4:]


def gradient(xt, c_all, xl):
    width = c_all.shape[1]

    def kernel(xl_ref, xt_ref, c_ref, own_ref, row_ref, col_ref, *others):
        g = jnp.dot(xt_ref[...], c_ref[...], preferred_element_type=F32) * float(TOKENS) ** (-0.5)
        own, other = own_other(g, xl_ref[0] == 0, 0)
        own_ref[...] = own
        for k, other_ref in enumerate(others):

            @pl.when(pl.program_id(0) == k)
            def _():
                other_ref[...] = other

        @pl.when(pl.program_id(0) == 0)
        def _():
            row_ref[...] = jnp.zeros_like(row_ref)

        squares_of(g, row_ref, col_ref, slice(None), False)

    out = pl.pallas_call(
        kernel,
        grid=(width // TILE,),
        out_shape=grad_shapes(width),
        in_specs=[
            pl.BlockSpec(memory_space=pltpu.SMEM),
            pl.BlockSpec((512, TOKENS), lambda j: (0, 0)),
            pl.BlockSpec((TOKENS, TILE), lambda j: (0, j)),
        ],
        out_specs=(
            pl.BlockSpec((256, TILE), lambda j: (0, j)),
            pl.BlockSpec((512, 128), lambda j: (0, 0)),
            pl.BlockSpec((8, TILE), lambda j: (0, j)),
        )
        + (pl.BlockSpec((256, TILE), lambda j: (0, 0)),) * (width // TILE),
        compiler_params=pltpu.CompilerParams(vmem_limit_bytes=56 * MIB),
        cost_estimate=LONG,
    )(xl, xt, c_all)
    return *out[:3], out[3:]


def terms(where, far, c_1, c_2, w_all, received=None):
    w1, w2 = c_1.shape[1], c_2.shape[1]
    keep = received is not None

    def kernel(where_ref, c1_ref, c2_ref, w_ref, *refs):
        t = jnp.dot(c1_ref[...], w_ref[:w1], preferred_element_type=F32)
        t = t + jnp.dot(c2_ref[...], w_ref[w1:], preferred_element_type=F32)
        if not keep:
            refs[0][...] = t
            return
        got_ref, both_1, both_2, own, other = refs
        t = t + got_ref[...]

        @pl.when(pl.program_id(0) == 0)
        def _():
            for ref, rows in ((both_1, t[:256]), (both_2, t[256:])):
                ref[:, :256], ref[:, 256:] = own_other(rows, where_ref[0] == 0, 1)

        @pl.when(pl.program_id(0) == 1)
        def _():
            own[...], other[...] = own_other(t, where_ref[0] == 0, 1)

    def rows(i, where_ref):
        high = 1 - where_ref[1] if far else where_ref[1]
        core = where_ref[2] if keep else 1 - where_ref[2]
        return ((2 * high + core) * 2 + i, 0)

    step = pl.BlockSpec((512, 512), lambda i, where_ref: (i, 0))
    block = jax.ShapeDtypeStruct((512, 256), F32)
    whole = [pl.BlockSpec(shape, lambda i, where_ref: (0, 0)) for shape in ((256, 512), (256, 512), (512, 256), (512, 256))]
    return pl.pallas_call(
        kernel,
        grid_spec=pltpu.PrefetchScalarGridSpec(
            num_scalar_prefetch=1,
            grid=(2,),
            in_specs=[
                pl.BlockSpec((512, w1), rows),
                pl.BlockSpec((512, w2), rows),
                pl.BlockSpec((w1 + w2, 512), lambda i, where_ref: (0, 0)),
            ]
            + [step] * keep,
            out_specs=whole if keep else step,
        ),
        out_shape=[jax.ShapeDtypeStruct((256, 512), F32)] * 2 + [block, block]
        if keep
        else jax.ShapeDtypeStruct((1024, 512), F32),
        compiler_params=pltpu.CompilerParams(vmem_limit_bytes=56 * MIB),
        cost_estimate=LONG,
    )(where, c_1, c_2, w_all, *((received,) if keep else ()))


def clipped(where, scale, row_factor, own, received, own_factors, received_factors):
    half = sum(g.shape[1] for g in own)
    tile = half // 2
    blocks = own + received
    firsts = [sum(g.shape[1] for g in blocks[:k]) for k in range(len(blocks))]

    def kernel(where_ref, scale_ref, row_ref, col_ref, *refs):
        out_ref = refs[-1]
        rows = row_ref[...] * scale_ref[0]
        for step in range(4):

            @pl.when(pl.program_id(0) == step)
            def _():
                for ref, first in zip(refs, firsts):
                    low, high = max(first, step * tile), min(first + ref.shape[1], (step + 1) * tile)
                    if low < high:
                        to = slice(low - step * tile, high - step * tile)
                        out_ref[:, to] = ref[:, low - first : high - first] * rows * col_ref[:, to]

    def place(j, where_ref):
        own_half = where_ref[0] + (j // 2) * (1 - 2 * where_ref[0])
        return (0, own_half * 2 + j % 2)

    return pl.pallas_call(
        kernel,
        grid_spec=pltpu.PrefetchScalarGridSpec(
            num_scalar_prefetch=1,
            grid=(4,),
            in_specs=[
                pl.BlockSpec(memory_space=pltpu.SMEM),
                pl.BlockSpec((256, 1), lambda j, where_ref: (0, 0)),
                pl.BlockSpec((1, tile), lambda j, where_ref: (0, j)),
            ]
            + [pl.BlockSpec(g.shape, lambda j, where_ref: (0, 0)) for g in blocks],
            out_specs=pl.BlockSpec((256, tile), place),
        ),
        out_shape=jax.ShapeDtypeStruct((256, 2 * half), F32),
        compiler_params=pltpu.CompilerParams(vmem_limit_bytes=56 * MIB),
        cost_estimate=LONG,
    )(
        where,
        scale.reshape(1),
        row_factor[:, None],
        jnp.concatenate([own_factors, received_factors])[None, :],
        *blocks,
    )


def body(tokens, cotangent, weight, row_prev, col_prev):
    y, z = lax.axis_index("y"), lax.axis_index("z")
    xl, xh, c = lax.axis_index("xl"), lax.axis_index("xh"), lax.axis_index("c")
    half = cotangent.shape[1] // 2
    first_xl = xl == 0
    after = lax.optimization_barrier

    where = jnp.stack([xl, xh, c]).astype(jnp.int32)

    away = mine(cotangent, half, 1, 1 - xl)
    part, away = after((mine(tokens, 32, 0, 2 * xh + c), away))
    other = lax.ppermute(away, "xl", SWAP)
    part = part.reshape(32, 16, 512)
    xo = lax.all_to_all(part, ("y", "z"), split_axis=1, concat_axis=0, tiled=False)

    own = mine(cotangent, half, 1, xl)
    row_prev_other = lax.ppermute(row_prev, "xl", SWAP)
    own, other, xo, row_prev_other = after((own, other, xo, row_prev_other))
    own_1, own_2 = own[:, :WIDE], own[:, WIDE:]
    other_1, other_2 = other[:, :WIDE], other[:, WIDE:]
    shard = jnp.where(first_xl, jnp.stack([own_2, other_2]), jnp.stack([other_2, own_2]))
    c_2 = lax.all_gather(shard, ("y", "z"), axis=0, tiled=False).reshape(TOKENS, half - WIDE)
    pair, near, far = first_pieces(own_1, near_three(own_1, "y"), "z")
    pair_2, near_2, far_2 = first_pieces(other_1, near_three(other_1, "z"), "y")

    to = lax.ppermute(xo, "c", SWAP)
    xs = [lax.ppermute(xo, "xl", SWAP), lax.ppermute(xo, "xh", SWAP), lax.ppermute(xo, ("xl", "xh"), DIAG)]
    xs, near, near_2 = after((xs, near, near_2))
    xt = transposed_tokens(where, xo, xs, to, lax.ppermute(jnp.stack(xs), "c", SWAP))
    pair, pair_2, xt = after((pair, pair_2, xt))
    pieces = pair + near + far + other_pieces(pair, "z") + pair_2 + near_2 + far_2 + other_pieces(pair_2, "y")
    index = [((y - dy) % 4 * 4 + (z - dz) % 4) * 2 + xl for dy, dz in PLACES]
    index += [((y - dy) % 4 * 4 + (z - dz) % 4) * 2 + 1 - xl for dz, dy in PLACES]
    w_own = mine(weight, half, 1, xl)
    w_other = lax.ppermute(mine(weight, half, 1, 1 - xl), "xl", SWAP)
    w_other, xt = after((w_other, xt))
    w_all = jnp.where(first_xl, jnp.concatenate([w_own, w_other]), jnp.concatenate([w_other, w_own])).T

    g_2, rows_2, cols_2, send_2 = gradient(xt, c_2, where)
    received_2 = [lax.ppermute(g, "xl", SWAP) for g in send_2]
    pieces, w_all, xt, rows_2 = after((pieces, w_all, xt, rows_2))
    c_1, g_1, rows_1, cols_1, send_1 = gradient_of_pieces(xt, pieces, jnp.stack(index).astype(jnp.int32), where)
    received_1 = [lax.ppermute(g, "xl", SWAP) for g in send_1]
    cols = jnp.sum(jnp.concatenate([cols_1, cols_2], 1), 0)
    w_all, received_2[0], cols = after((w_all, received_2[0], cols))
    col_sum = jnp.sum(spread(cols, ("y", "z"), 16), 0)
    far_terms = terms(where, True, c_1, c_2, w_all)
    far_core = lax.ppermute(far_terms, "c", SWAP)
    far_terms, received_1[0], col_sum, w_all = after((far_terms, received_1[0], col_sum, w_all))

    col_prev_mine = mine(col_prev, half, 0, xl)
    col_half = decay_rate * col_prev_mine + (1.0 - decay_rate) * (col_sum / D + tiny_eps)
    near_terms = terms(where, False, c_1, c_2, w_all)
    near_core = lax.ppermute(near_terms, "c", SWAP)
    near_terms, far_core, received_1[1] = after((near_terms, far_core, received_1[1]))

    def over_columns(g, col):
        return jnp.sum(g * g * (1.0 / col)[None, :], 1)

    col_1, col_2 = col_half[:WIDE], col_half[WIDE:]
    over_own = over_columns(g_1, col_1) + over_columns(g_2, col_2)
    over_other, first = 0.0, 0
    for g in send_1 + send_2:
        over_other = over_other + over_columns(g, col_half[first : first + g.shape[1]])
        first += g.shape[1]
    plain = jnp.sum(rows_1 + rows_2, 1)
    plain_own, plain_other = own_other(plain, first_xl, 0)
    sums = jnp.stack([plain_own, over_own, plain_other, over_other])
    give_1, give_2, far_give, far_keep = terms(where, True, c_1, c_2, w_all, far_core)
    seen = spread(sums, ("xl", "xh", "c"), 8).reshape(2, 4, 4, 256)
    got_1 = lax.ppermute(give_1, ("xl", "xh"), DIAG)
    got_far = lax.ppermute(far_give, "xl", SWAP)
    keep_1, keep_2, own_b, give_b = terms(where, False, c_1, c_2, w_all, near_core)
    seen, far_keep, received_2[1], keep_1, give_b = after((seen, far_keep, received_2[1], keep_1, give_b))
    same = jnp.sum(jnp.where(first_xl, seen[0], seen[1]), 0)
    cross = jnp.sum(jnp.where(first_xl, seen[1], seen[0]), 0)
    row_sum = jnp.concatenate([same[0] + cross[2], same[2] + cross[0]])
    row_over = jnp.concatenate([same[1] + cross[3], same[3] + cross[1]])
    row_prev_two = jnp.concatenate([row_prev, row_prev_other])
    row_next = decay_rate * row_prev_two + (1.0 - decay_rate) * (row_sum / FF + tiny_eps)
    row_own = row_next[:256]

    lane = lax.broadcasted_iota(jnp.int32, (128,), 0)
    pair = jnp.where(lane == 0, jnp.sum(row_over / row_next), jnp.where(lane == 1, jnp.sum(row_next), 0.0))
    totals = spread(pair, ("y", "z"), 16)
    got_2 = lax.ppermute(give_2, ("xl", "xh"), DIAG)
    col_other = lax.ppermute(col_half, "xl", SWAP)
    got_b = lax.ppermute(give_b, "xl", SWAP)
    totals, col_other, got_1, got_far, got_2 = after((totals, col_other, got_1, got_far, got_2))
    totals = jnp.sum(totals, 0)
    last_b = lax.ppermute(far_keep + got_far, ("xl", "xh"), DIAG)
    keep_a, got_a = jnp.concatenate([keep_1, keep_2]), jnp.concatenate([got_1, got_2])
    last_a = lax.ppermute(keep_a[:, 256:] + got_a[:, :256], "xl", SWAP)
    row_mean = totals[1] / D
    update_rms = jnp.sqrt(row_mean * (totals[0] / (D * FF)))
    scale = jnp.sqrt(row_mean) / jnp.maximum(1.0, update_rms)
    update = clipped(
        where,
        scale,
        1.0 / jnp.sqrt(row_own),
        (g_1, g_2),
        (*received_1, *received_2),
        1.0 / jnp.sqrt(col_half),
        1.0 / jnp.sqrt(col_other),
    )
    col_next = jnp.where(
        first_xl, jnp.concatenate([col_half, col_other]), jnp.concatenate([col_other, col_half])
    )

    total_a = (keep_a[:, :256] + got_a[:, 256:]) + last_a
    total_b = (own_b + got_b) + last_b
    total = jnp.concatenate([total_a.astype(BF16), total_b.astype(BF16)])

    return (total, update, row_own, col_next, update_rms)


def solution(mesh):
    fine = Mesh(mesh.devices.reshape(SIZES), AXES)
    fsdp, mp = ("y", "z", "xl"), ("xh", "c")
    in_specs = (P(fsdp, None), P(fsdp, mp), P(fsdp, mp), P(fsdp), P(mp))
    out_specs = (P(mp, fsdp), P(fsdp, mp), P(fsdp), P(mp), P())
    return jax.shard_map(body, mesh=fine, in_specs=in_specs, out_specs=out_specs, check_vma=False)
```
